256 devices in a mesh: group: 16 (over x, z_hi), member: 16 (over y, z_lo, core).
Axes of the slice: x: 4, y: 4, z: 8 (z_hi: 4, z_lo: 2; z = z_hi * 2 + z_lo), core: 2. Of those that a mesh axis runs over, the one named last changes fastest.
Arguments:
- prompt_k: bfloat16 [16, 1024, 1024], P('group', 'member'), may hold values from -6 to 6
- prompt_v: bfloat16 [16, 1024, 1024], P('group', 'member'), may hold values from -18 to 18
- resp_q: bfloat16 [16, 16, 128, 4096], P('group', 'member'), may hold values from -45 to 45
- resp_k: bfloat16 [16, 16, 128, 1024], P('group', 'member'), may hold values from -6 to 6
- resp_v: bfloat16 [16, 16, 128, 1024], P('group', 'member'), may hold values from -18 to 18
- out_grad: bfloat16 [16, 16, 128, 4096], P('group', 'member'), may hold values from -6 to 6
- lengths: int32 [16, 16], P('group', 'member'), may hold values from 16 to 128, as said below
- rewards: float32 [16, 16], P('group', 'member'), may hold values from -6 to 6
Outputs:
- attended: bfloat16 [16, 16, 128, 4096], P('group', 'member')
- grad_q: bfloat16 [16, 16, 128, 4096], P('group', 'member')
- grad_resp_k: bfloat16 [16, 16, 128, 1024], P('group', 'member')
- grad_resp_v: bfloat16 [16, 16, 128, 1024], P('group', 'member')
- grad_prompt_k: bfloat16 [16, 1024, 1024], P('group', 'member')
- grad_prompt_v: bfloat16 [16, 1024, 1024], P('group', 'member')
The draws below stay inside these ranges and needn't reach their ends.
Inputs may be any that keep to these rules, and one draw needn't show every extreme that they name: In each group the lengths never fall from one member to the next, and the last member's response has exactly 128 live tokens.
All inputs are finite; a program needn't handle non-finite values.
Results may differ from the reference program's by a relative error of at most 0.0082.
Values may be sent and summed in bfloat16 or wider, within the bound.
No kernel may reach another device: no remote copies, remote signals or barrier semaphores. Data moves between devices by JAX's collectives and lax.ppermute only.
A program may use at most 128 MiB of HBM per device.

```python
import jax
import jax.numpy as jnp
from jax import lax

H = 32
KVH = 8
HD = 128
CAP = 128
GROUPS = 16
RESP = 16
PROMPT = 1024


def draw_prompt_k(key, part):
    key = jax.random.fold_in(key, 1)
    full_shape = (GROUPS, PROMPT, KVH * HD)
    return jnp.clip(jax.random.normal(key, full_shape, jnp.float32), -6.0, 6.0).astype(jnp.bfloat16)


def draw_resp_q(key, part):
    key = jax.random.fold_in(key, 2)
    full_shape = (GROUPS, RESP, CAP, H * HD)
    return jnp.clip(2.0 * jax.random.normal(key, full_shape, jnp.float32), -12.0, 12.0).astype(jnp.bfloat16)


def draw_lengths(key, part):
    key = jax.random.fold_in(key, 3)
    lowest = max(1, CAP // 8)
    drawn = jax.random.randint(key, (GROUPS, RESP), lowest, CAP + 1, jnp.int32)
    drawn = jnp.sort(drawn, axis=1)
    return drawn.at[:, RESP - 1].set(CAP)


def block_scale(key, dims, cuts, least, largest):
    factor_of, own = 1.0, jax.random.fold_in(key, 6)
    for dim, parts in cuts:
        heights = jnp.exp(jax.random.uniform(jax.random.fold_in(own, dim), (parts,), jnp.float32, least / len(cuts), largest / len(cuts)))
        factor_of = factor_of * jnp.repeat(heights, dims[dim] // parts).reshape([-1 if axis == dim else 1 for axis in range(len(dims))])
    return factor_of


def scatter_about(key, shape, spread, limit, cuts=(), held_as=jnp.bfloat16):
    factor_of = block_scale(key, shape, cuts, -0.22, 0.18) if cuts else 1.0
    result = jax.random.normal(key, shape, jnp.float32) * spread * factor_of
    return jnp.minimum(jnp.maximum(result, -limit), limit).astype(held_as)


def setup_inputs(seed: int = 0) -> dict:
    keys = jax.random.split(jax.random.key(seed), 9)
    prompt_k = draw_prompt_k(jax.random.fold_in(keys[8], 71), 0)
    prompt_v = scatter_about(keys[1], (GROUPS, PROMPT, KVH * HD), 3.0, 18.0, ((0, 16), (1, 16)))
    resp_q = draw_resp_q(jax.random.fold_in(keys[8], 71), 0)
    resp_k = scatter_about(keys[3], (GROUPS, RESP, CAP, KVH * HD), 1.0, 6.0, ((0, 16), (1, 16)))
    resp_v = scatter_about(keys[4], (GROUPS, RESP, CAP, KVH * HD), 3.0, 18.0, ((0, 16), (1, 16)))
    out_grad = scatter_about(keys[5], (GROUPS, RESP, CAP, H * HD), 1.0, 6.0, ((0, 16), (1, 16)))
    lengths = draw_lengths(jax.random.fold_in(keys[8], 71), 0)
    rewards = scatter_about(keys[7], (GROUPS, RESP), 1.0, 6.0, ((0, 16), (1, 16)), jnp.float32)
    return dict(prompt_k=prompt_k, prompt_v=prompt_v, resp_q=resp_q, resp_k=resp_k, resp_v=resp_v, out_grad=out_grad, lengths=lengths, rewards=rewards)


def to_heads(rows_in, kv_heads, head_size):
    row_count = rows_in.shape[0]
    per_head = rows_in.shape[1] // (kv_heads * head_size)
    shaped = rows_in.reshape(row_count, kv_heads, per_head, head_size)
    return shaped.transpose(1, 2, 0, 3).reshape(kv_heads, per_head * row_count, head_size)


def from_heads(blocks, row_count):
    kv_heads, rows_all, head_size = blocks.shape
    per_head = rows_all // row_count
    shaped = blocks.reshape(kv_heads, per_head, row_count, head_size)
    return shaped.transpose(2, 0, 1, 3).reshape(row_count, kv_heads * per_head * head_size)


def head_terms(queries, cotangent, all_keys, all_values, allowed, first_key, score_scale):
    scores = jnp.dot(queries, all_keys.T, preferred_element_type=jnp.float32) * score_scale
    scores = jnp.where(allowed, scores, -jnp.inf)
    row_max = jnp.max(scores, axis=1, keepdims=True)
    raised = jnp.exp(scores - row_max)
    row_sum = jnp.sum(raised, axis=1, keepdims=True)
    probability = raised / row_sum
    probs_low = probability.astype(jnp.bfloat16)
    output = jnp.dot(probs_low, all_values, preferred_element_type=jnp.float32)
    dprobs = jnp.dot(cotangent, all_values.T, preferred_element_type=jnp.float32)
    row_delta = jnp.sum(cotangent.astype(jnp.float32) * output, axis=1, keepdims=True)
    dscores = (probability * (dprobs - row_delta)).astype(jnp.bfloat16)
    grad_query = jnp.dot(dscores, all_keys, preferred_element_type=jnp.float32) * score_scale
    grad_keys = jnp.dot(dscores[:, first_key:].T, queries, preferred_element_type=jnp.float32) * score_scale
    grad_values = jnp.dot(probs_low[:, first_key:].T, cotangent, preferred_element_type=jnp.float32)
    return output, grad_query, grad_keys, grad_values, row_max, row_sum, row_delta


def reference(prompt_k, prompt_v, resp_q, resp_k, resp_v, out_grad, lengths, rewards):
    score_scale = float(HD) ** -0.5
    token_total = jnp.sum(lengths.astype(jnp.float32))
    factor = jnp.float32(CAP * GROUPS * RESP) / token_total
    advantage = rewards - jnp.sum(rewards, axis=1, keepdims=True) / RESP
    position = jnp.arange(CAP)
    per_head = H // KVH
    row_pos = jnp.tile(position, per_head)
    key_pos = jnp.arange(PROMPT + CAP)
    allowed = (key_pos[None, :] < PROMPT) | (key_pos[None, :] - PROMPT <= row_pos[:, None])

    def one_group(group_inputs):
        group_k, group_v, queries_all, rkeys_all, rvalues_all, upstream_all, length_all, advantage_all = group_inputs

        def one_response(carry, inputs):
            queries, rkeys, rvalues, upstream, length, adv_one = inputs
            live_rows = position < length
            weight = jnp.where(live_rows, adv_one * factor, 0.0).astype(jnp.float32)
            cotangent = (upstream.astype(jnp.float32) * weight[:, None]).astype(jnp.bfloat16)
            all_keys = jnp.concatenate([group_k, rkeys], axis=0)
            all_values = jnp.concatenate([group_v, rvalues], axis=0)
            operands = (to_heads(queries, KVH, HD), to_heads(cotangent, KVH, HD),
                        to_heads(all_keys, KVH, HD), to_heads(all_values, KVH, HD))

            def per_kv_head(head_ops):
                return head_terms(head_ops[0], head_ops[1], head_ops[2], head_ops[3], allowed, 0, score_scale)

            output, grad_query, grad_keys, grad_values, row_max, row_sum, row_delta = lax.map(per_kv_head, operands)
            attended = (from_heads(output, CAP) * live_rows[:, None]).astype(jnp.bfloat16)
            grad_q = from_heads(grad_query, CAP).astype(jnp.bfloat16)
            key_rows = from_heads(grad_keys, PROMPT + CAP)
            value_rows = from_heads(grad_values, PROMPT + CAP)
            carry = (carry[0] + key_rows[:PROMPT], carry[1] + value_rows[:PROMPT])
            return carry, (attended, grad_q, key_rows[PROMPT:].astype(jnp.bfloat16), value_rows[PROMPT:].astype(jnp.bfloat16))

        zeros_init = jnp.zeros((PROMPT, KVH * HD), jnp.float32)
        sums, outputs = lax.scan(one_response, (zeros_init, zeros_init),
                                 (queries_all, rkeys_all, rvalues_all, upstream_all, length_all, advantage_all))
        return outputs + (sums[0].astype(jnp.bfloat16), sums[1].astype(jnp.bfloat16))

    results = lax.map(one_group, (prompt_k, prompt_v, resp_q, resp_k, resp_v, out_grad, lengths, advantage))
    return results[0], results[1], results[2], results[3], results[4], results[5]
```

```python
import functools

import jax
import jax.numpy as jnp
from jax import lax
from jax.experimental import pallas as pl
from jax.experimental.pallas import tpu as pltpu
from jax.sharding import Mesh
from jax.sharding import PartitionSpec as P

BF16 = jnp.bfloat16
F32 = jnp.float32
KVH = 8
HD = 128
LOG2E = 1.4426950408889634
NT = (((1,), (1,)), ((), ()))
NN = (((1,), (0,)), ((), ()))


def dot(a, b, dims=NN):
    return lax.dot_general(a, b, dims, preferred_element_type=F32)


def step(values, axis, by):
    size = lax.axis_size(axis)
    return lax.ppermute(values, axis, [(i, (i + by) % size) for i in range(size)])


def heads_to_rows(wide):
    return jnp.concatenate([wide[:, i * HD : (i + 1) * HD] for i in range(wide.shape[1] // HD)], axis=0)


def response_terms(queries, upstream, length, advantage, keys, values, keys_t, values_t, scale):
    slots = queries.shape[0]
    prompt_len = keys.shape[0] - slots
    token = lax.broadcasted_iota(jnp.int32, (slots, HD), 0).astype(F32)
    live = token < length
    weight = jnp.where(live, jnp.broadcast_to(advantage, live.shape), 0.0)
    per_head = queries.shape[1] // HD
    q_rows = heads_to_rows(queries)
    cot = [(upstream[:, i * HD : (i + 1) * HD].astype(F32) * weight).astype(BF16) for i in range(per_head)]
    cot_rows = jnp.concatenate(cot, axis=0)
    rows = q_rows.shape[0]
    scores = dot(keys, q_rows, NT)
    key_pos = lax.broadcasted_iota(jnp.int32, (slots, rows), 0)
    row_pos = lax.broadcasted_iota(jnp.int32, (slots, rows), 1) % slots
    tail = jnp.where(key_pos <= row_pos, scores[prompt_len:], -jnp.inf)
    scores = jnp.concatenate([scores[:prompt_len], tail], axis=0)
    row_max = jnp.max(scores, axis=0, keepdims=True)
    raised = jnp.exp2((scores - row_max) * (scale * LOG2E))
    row_sum = jnp.sum(raised, axis=0, keepdims=True)
    probs = raised * (1.0 / row_sum)
    probs_low = probs.astype(BF16)
    output_t = dot(values_t, probs_low)
    dprobs = dot(values, cot_rows, NT)
    cot_t = cot_rows.astype(F32).T
    delta = jnp.sum(cot_t * output_t, axis=0, keepdims=True)
    dscores = (probs * (dprobs - delta)).astype(BF16)
    grad_q_t = dot(keys_t, dscores) * scale
    grad_keys = dot(dscores, q_rows) * scale
    grad_values = dot(probs_low, cot_rows)
    attended = [jnp.where(live, output_t[:, i * slots : (i + 1) * slots].T, 0.0).astype(BF16) for i in range(per_head)]
    grad_q = [grad_q_t[:, i * slots : (i + 1) * slots].T.astype(BF16) for i in range(per_head)]
    return attended, grad_q, grad_keys, grad_values


def attention_kernel(scale, side_ref, *refs):
    blocks, far, far_z = refs[:6], refs[6:8], refs[8:10]
    q_own, g_own, k_own, v_own, q_sib, g_sib, k_sib, v_sib = refs[10:18]
    att_out, gq_out, gk_out, gv_out, sib_out = refs[18:23]
    parts = refs[23:31]
    keys_scr, values_scr = refs[31:33]
    slots = q_own.shape[2]
    rows = far[0].shape[0]
    per_head = q_own.shape[3] // HD
    held = [(b[0:rows], b[rows : 2 * rows], b[2 * rows :]) for b in blocks]
    held[4:4] = [(far[0][...], far[1][0:rows], far[1][rows:])]
    held.append((far_z[0][...], far_z[1][0:rows], far_z[1][rows:]))
    for i, (k, v, _) in enumerate(held):
        keys_scr[i * rows : (i + 1) * rows] = k
        values_scr[i * rows : (i + 1) * rows] = v
    prompt_len = len(held) * rows
    facts = [scal.astype(F32) for _, _, scal in held]
    total = sum(facts[1:], facts[0])
    members = 2.0 * len(held)
    reward = lambda f, at: f[at + 1 : at + 2] + f[at + 2 : at + 3] + f[at + 3 : at + 4]
    reward_mean = (reward(total, 0) + reward(total, 8)) * (1.0 / members)

    grads = []
    for at, q, g, rk, rv in ((0, q_own[0, 0], g_own[0, 0], k_own[0, 0], v_own[0, 0]), (8, q_sib[...], g_sib[...], k_sib[...], v_sib[...])):
        keys_scr[prompt_len:] = rk
        values_scr[prompt_len:] = rv
        keys, values = keys_scr[...], values_scr[...]
        length = facts[0][at : at + 1]
        advantage = reward(facts[0], at) - reward_mean
        attended, grad_q, grad_keys, grad_values = response_terms(
            q, g, length, advantage, keys, values, keys.T, values.T, scale
        )
        gk, gv = grad_keys[prompt_len:].astype(BF16), grad_values[prompt_len:].astype(BF16)
        for i in range(per_head):
            cols = slice(i * HD, (i + 1) * HD)
            if at == 0:
                att_out[0, 0, :, cols] = attended[i]
                gq_out[0, 0, :, cols] = grad_q[i]
            else:
                sib_out[:, cols] = attended[i]
                sib_out[:, (per_head + i) * HD : (per_head + i + 1) * HD] = grad_q[i]
        if at == 0:
            gk_out[0, 0] = gk
            gv_out[0, 0] = gv
        else:
            sib_out[:, 2 * per_head * HD : (2 * per_head + 1) * HD] = gk
            sib_out[:, (2 * per_head + 1) * HD :] = gv
        grads.append((grad_keys, grad_values))
    grad_keys = grads[0][0][:prompt_len] + grads[1][0][:prompt_len]
    grad_values = grads[0][1][:prompt_len] + grads[1][1][:prompt_len]
    for i, part in enumerate(parts):
        part[0:rows] = grad_keys[i * rows : (i + 1) * rows].astype(part.dtype)
        part[rows:] = grad_values[i * rows : (i + 1) * rows].astype(part.dtype)


def attention(side, blocks, far, far_z, resp_q, out_grad, resp_k, resp_v, packed, kv_heads):
    _, _, slots, width = resp_q.shape
    rows = far[0].shape[0]
    per_head = width // (KVH * HD)
    wide = per_head * HD
    whole = lambda a: pl.BlockSpec((a.shape[0], HD), lambda h, s: (0, h))
    own = lambda w: pl.BlockSpec((1, 1, slots, w), lambda h, s: (0, 0, 0, s[0] * kv_heads + h))
    at = lambda w, first: pl.BlockSpec((slots, w), lambda h, s: (0, first + h))
    in_specs = [whole(a) for a in (*blocks, *far, *far_z)]
    in_specs += [own(wide), own(wide), own(HD), own(HD)]
    in_specs += [at(wide, 0), at(wide, kv_heads), at(HD, 2 * kv_heads * per_head), at(HD, 2 * kv_heads * per_head + kv_heads)]
    sib_wide = 2 * wide + 2 * HD
    out_specs = [own(wide), own(wide), own(HD), own(HD), at(sib_wide, 0)]
    out_shape = [jax.ShapeDtypeStruct(a.shape, BF16) for a in (resp_q, out_grad, resp_k, resp_v)]
    out_shape.append(jax.ShapeDtypeStruct((slots, kv_heads * sib_wide), BF16))
    for i in range(8):
        out_specs.append(pl.BlockSpec((2 * rows, HD), lambda h, s: (0, h)))
        out_shape.append(jax.ShapeDtypeStruct((2 * rows, kv_heads * HD), F32 if i == 0 else BF16))
    keys = 8 * rows + slots
    return pl.pallas_call(
        functools.partial(attention_kernel, float(HD) ** -0.5),
        grid_spec=pltpu.PrefetchScalarGridSpec(
            num_scalar_prefetch=1,
            grid=(kv_heads,),
            in_specs=in_specs,
            out_specs=out_specs,
            scratch_shapes=[pltpu.VMEM((keys, HD), BF16), pltpu.VMEM((keys, HD), BF16)],
        ),
        out_shape=out_shape,
        compiler_params=pltpu.CompilerParams(vmem_limit_bytes=56 * 2**20),
        cost_estimate=pl.CostEstimate(flops=7_000_000_000, bytes_accessed=16_000_000, transcendentals=5_000_000),
    )(side, *blocks, *far, *far_z, resp_q, out_grad, resp_k, resp_v, packed, packed, packed, packed)


def body(prompt_k, prompt_v, resp_q, resp_k, resp_v, out_grad, lengths, rewards):
    side = lax.axis_index("core")
    other = 1 - side
    slots, width = resp_q.shape[2:]
    kv_heads = KVH // 2
    half = prompt_k.shape[2] // 2
    rows = prompt_k.shape[1]
    devices = 1
    for axis in ("x", "zh", "y", "zl", "core"):
        devices *= lax.axis_size(axis)

    reward = rewards[0, 0]
    high = lax.reduce_precision(reward, 8, 7)
    middle = lax.reduce_precision(reward - high, 8, 7)
    low = reward - high - middle
    facts = jnp.stack([lengths[0, 0].astype(F32), high, middle, low, 0.0, 0.0, 0.0, 0.0])
    facts = jnp.broadcast_to(facts[:, None], (8, half)).astype(BF16)

    def half_of(a, which):
        return lax.dynamic_slice_in_dim(a, which * (a.shape[1] // 2), a.shape[1] // 2, 1)

    my_k, my_v = half_of(prompt_k[0], side), half_of(prompt_v[0], side)
    give = jnp.concatenate([half_of(prompt_k[0], other), half_of(prompt_v[0], other), facts, facts], axis=0)
    got = step(give, "core", 1)
    mine = jnp.concatenate([my_k, got[:rows], my_v, got[rows : 2 * rows], facts, got[2 * rows : 2 * rows + 8]], axis=0)
    packed = jnp.concatenate([half_of(a[0, 0], other) for a in (resp_q, out_grad, resp_k, resp_v)], axis=1)
    packed = step(packed, "core", 1)

    pair = 2 * rows
    near_z = step(mine, "zl", 1)
    below = step(mine, "y", 1)
    above = step(mine, "y", -1)
    below_z = step(near_z, "y", 1)
    above_z = step(near_z, "y", -1)
    far = (step(below[:pair], "y", 1), step(above[pair:], "y", -1))
    far_z = (step(far[0], "zl", 1), step(far[1], "zl", 1))

    tokens = sum(b[2 * pair : 2 * pair + 1, :HD].astype(F32) + b[2 * pair + 8 : 2 * pair + 9, :HD].astype(F32)
                 for b in (mine, near_z, below, above, below_z, above_z))
    tokens += sum(b[pair : pair + 1, :HD].astype(F32) + b[pair + 8 : pair + 9, :HD].astype(F32) for b in (far[1], far_z[1]))

    outs = attention(
        side.reshape(1).astype(jnp.int32),
        (mine, near_z, above, below, above_z, below_z),
        far, far_z, resp_q, out_grad, resp_k, resp_v, packed, kv_heads,
    )
    attended, grad_q, grad_rk, grad_rv, for_sib = outs[:5]
    p_own, p_near, p_above, p_below, p_far, p_above_z, p_below_z, p_far_z = outs[5:]

    for axis in ("x", "zh"):
        tokens = tokens + sum(step(tokens, axis, by) for by in range(1, lax.axis_size(axis)))
    factor = jnp.float32(slots * devices) / tokens[0, 0]

    def added(*terms):
        return sum(t.astype(F32) for t in terms).astype(BF16)

    from_z = step(p_far_z, "zl", 1)
    from_below = step(p_above_z, "y", 1)
    from_above = step(p_below_z, "y", -1)
    from_sib = step(for_sib, "core", 1)
    far_sum = added(p_far, from_z)
    near_sum = added(p_near, from_below, from_above)
    far_k = step(far_sum[:pair], "y", 1)
    far_v = step(far_sum[pair:], "y", -1)
    above_sum = jnp.concatenate([added(p_above[:pair], far_k), p_above[pair:]], axis=0)
    below_sum = jnp.concatenate([p_below[:pair], added(p_below[pair:], far_v)], axis=0)
    last = (step(near_sum, "zl", 1), step(above_sum, "y", 1), step(below_sum, "y", -1))
    total = p_own + sum(t.astype(F32) for t in last)
    total = total * factor
    keep = jnp.concatenate([total[:rows], total[pair : pair + rows]], axis=1).astype(BF16)
    pass_on = jnp.concatenate([total[rows:pair], total[pair + rows :]], axis=1).astype(BF16)
    passed = step(pass_on, "core", 1)

    def merge(own, got):
        return jnp.where(side == 0, jnp.concatenate([own, got], axis=1), jnp.concatenate([got, own], axis=1))

    sib_heads = from_sib.reshape(slots, kv_heads, -1)
    wide = width // KVH
    def fill(buffer, got, scaled):
        got = got.reshape(slots, -1)
        whole = lax.dynamic_update_slice(buffer[0, 0], got, (0, other * got.shape[1]))
        if scaled:
            whole = (whole.astype(F32) * factor).astype(BF16)
        return whole[None, None]

    attended = fill(attended, sib_heads[:, :, :wide], False)
    grad_q = fill(grad_q, sib_heads[:, :, wide : 2 * wide], True)
    grad_rk = fill(grad_rk, sib_heads[:, :, 2 * wide : 2 * wide + HD], True)
    grad_rv = fill(grad_rv, sib_heads[:, :, 2 * wide + HD :], True)
    grad_pk = merge(keep[:, :half], passed[:, :half])[None]
    grad_pv = merge(keep[:, half:], passed[:, half:])[None]
    return attended, grad_q, grad_rk, grad_rv, grad_pk, grad_pv


def solution(mesh):
    parts = Mesh(mesh.devices.reshape(4, 4, 4, 2, 2), ("x", "zh", "y", "zl", "core"))
    group, member = ("x", "zh"), ("y", "zl", "core")
    rank3, rank4, rank2 = P(group, member, None), P(group, member, None, None), P(group, member)
    return jax.shard_map(
        body,
        mesh=parts,
        in_specs=(rank3, rank3, rank4, rank4, rank4, rank4, rank2, rank2),
        out_specs=(rank4, rank4, rank4, rank4, rank3, rank3),
        check_vma=False,
    )
```

```python
import functools

import jax
import jax.numpy as jnp
from jax import lax
from jax.experimental import pallas as pl
from jax.experimental.pallas import tpu as pltpu
from jax.sharding import Mesh
from jax.sharding import PartitionSpec as P

BF16 = jnp.bfloat16
F32 = jnp.float32
KVH = 8
HD = 128
S_BLOCK, BLOCK, O_BLOCK, D_BLOCK = 384, 128, 1152, 384
VMEM = 40 * 2**20
LOG2E = 1.4426950408889634
NT = (((1,), (1,)), ((), ()))
NN = (((1,), (0,)), ((), ()))


def dot(a, b, dims=NN):
    return lax.dot_general(a, b, dims, preferred_element_type=F32)


def step(values, axis, by):
    size = lax.axis_size(axis)
    return lax.ppermute(values, axis, [(i, (i + by) % size) for i in range(size)])


def heads_to_rows(wide):
    return jnp.concatenate([wide[:, i * HD : (i + 1) * HD] for i in range(wide.shape[1] // HD)], axis=0)


def tree(op, parts):
    while len(parts) > 1:
        parts = [op(*parts[i : i + 2]) if i + 1 < len(parts) else parts[i] for i in range(0, len(parts), 2)]
    return parts[0]


def response_steps(facts, queries, upstream, keys, values, keys_t, values_t, e_scr, p_scr, d_scr, q_all, c_all, cols, att, grad, scale):
    length, advantage = facts
    slots = queries.shape[0]
    key_count = e_scr.shape[0]
    prompt_len = key_count - slots
    token = lax.broadcasted_iota(jnp.int32, (slots, HD), 0).astype(F32)
    live = token < length
    weight = jnp.where(live, jnp.broadcast_to(advantage, live.shape), 0.0)
    per_head = queries.shape[1] // HD
    q_rows = heads_to_rows(queries)
    cot = [(upstream[:, i * HD : (i + 1) * HD].astype(F32) * weight).astype(BF16) for i in range(per_head)]
    cot_rows = jnp.concatenate(cot, axis=0)
    q_all[cols] = q_rows
    c_all[cols] = cot_rows
    groups = lambda a: [a[i : i + 8] for i in range(0, a.shape[0], 8)]
    tops, sums = [], []
    for first in range(0, key_count, S_BLOCK):
        scores = dot(keys[first : first + S_BLOCK], q_rows, NT)
        if first + S_BLOCK > prompt_len:
            key_pos = lax.broadcasted_iota(jnp.int32, scores.shape, 0) + (first - prompt_len)
            row_pos = lax.broadcasted_iota(jnp.int32, scores.shape, 1) % slots
            scores = jnp.where(key_pos <= row_pos, scores, -jnp.inf)
        e_scr[first : first + S_BLOCK] = scores
        tops.append(tree(jnp.maximum, groups(scores)))
        yield
    yield "S"
    row_max = jnp.max(tree(jnp.maximum, tops), axis=0, keepdims=True) * (scale * LOG2E)
    for first in range(0, key_count, BLOCK):
        raised = jnp.exp2(e_scr[first : first + BLOCK] * (scale * LOG2E) - row_max)
        e_scr[first : first + BLOCK] = raised
        sums.append(tree(jnp.add, groups(raised)))
        yield
    yield "E"
    inverse = 1.0 / jnp.sum(tree(jnp.add, sums), axis=0, keepdims=True)
    output_t = None
    for first in range(0, key_count, O_BLOCK):
        for at in range(first, first + O_BLOCK, BLOCK):
            p_scr[at : at + BLOCK, cols] = (e_scr[at : at + BLOCK] * inverse).astype(BF16)
        term = dot(values_t[:, first : first + O_BLOCK], p_scr[first : first + O_BLOCK, cols])
        output_t = term if output_t is None else output_t + term
        yield
    yield "O"
    cot_t = cot_rows.astype(F32).T
    delta = jnp.sum(cot_t * output_t, axis=0, keepdims=True)
    for i in range(per_head):
        att[:, i * HD : (i + 1) * HD] = jnp.where(live, output_t[:, i * slots : (i + 1) * slots].T, 0.0).astype(BF16)
    for first in range(0, key_count, D_BLOCK):
        dprobs = dot(values[first : first + D_BLOCK], cot_rows, NT)
        probs = e_scr[first : first + D_BLOCK] * inverse
        d_scr[first : first + D_BLOCK, cols] = (probs * (dprobs - delta)).astype(BF16)
        yield
    yield "D"
    grad_q_t = dot(keys_t[...], d_scr[:, cols]) * scale
    for i in range(per_head):
        grad[:, i * HD : (i + 1) * HD] = grad_q_t[:, i * slots : (i + 1) * slots].T.astype(BF16)
    wide = per_head * HD
    grad[:, wide : wide + HD] = (dot(d_scr[prompt_len:, cols], q_rows) * scale).astype(BF16)
    grad[:, wide + HD :] = dot(p_scr[prompt_len:, cols], cot_rows).astype(BF16)
    yield "G"


def run(steps, until):
    for mark in steps:
        yield
        if mark == until:
            return


def turns(*runs):
    runs = list(runs)
    while runs:
        for r in list(runs):
            try:
                next(r)
            except StopIteration:
                runs.remove(r)


def prep_kernel(k_in, v_in, length_in, reward_in, keep, give, side_out):
    rows, width = k_in.shape[1:]
    half = width // 2
    reward = jnp.broadcast_to(reward_in[...], (16, half))
    length = jnp.broadcast_to(length_in[...].astype(F32), (16, half))
    high = reward.astype(BF16).astype(F32)
    middle = (reward - high).astype(BF16).astype(F32)
    row = lax.broadcasted_iota(jnp.int32, (16, half), 0) % 8
    facts = length
    for at, value in ((1, high), (2, middle), (3, reward - high - middle)):
        facts = jnp.where(row == at, value, facts)
    facts = jnp.where(row < 4, facts, 0.0).astype(BF16)

    def write(mine, other):
        for out, cols in ((mine, slice(0, half)), (other, slice(half, width))):
            out[0:rows] = k_in[0, :, cols]
            out[rows : 2 * rows] = v_in[0, :, cols]
            out[2 * rows :] = facts

    side = lax.axis_index("core")
    side_out[0] = side.astype(jnp.int32)
    pl.when(side == 0)(lambda: write(keep, give))
    pl.when(side != 0)(lambda: write(give, keep))


def prep(prompt_k, prompt_v, lengths, rewards):
    _, rows, width = prompt_k.shape
    whole = lambda shape: pl.BlockSpec(shape, lambda i: (0,) * len(shape))
    out = jax.ShapeDtypeStruct((2 * rows + 16, width // 2), BF16)
    return pl.pallas_call(
        prep_kernel,
        grid=(1,),
        in_specs=[whole(a.shape) for a in (prompt_k, prompt_v, lengths, rewards)],
        out_specs=[whole(out.shape), whole(out.shape), pl.BlockSpec(memory_space=pltpu.SMEM)],
        out_shape=[out, out, jax.ShapeDtypeStruct((1,), jnp.int32)],
        cost_estimate=pl.CostEstimate(flops=0, bytes_accessed=500_000, transcendentals=0),
        name="prep",
    )(prompt_k, prompt_v, lengths, rewards)


def pack_kernel(side_ref, *refs):
    inputs, out, sems = refs[:4], refs[4], refs[5]
    other = 1 - side_ref[0]
    copies, first = [], 0
    for i, a in enumerate(inputs):
        half = a.shape[3] // 2
        source = a.at[0, 0, :, pl.ds(pl.multiple_of(other * half, HD), half)]
        copies.append(pltpu.make_async_copy(source, out.at[:, first : first + half], sems.at[i]))
        first += half
    for copy in copies:
        copy.start()
    for copy in copies:
        copy.wait()


def pack(side, *inputs):
    width = sum(a.shape[3] for a in inputs) // 2
    return pl.pallas_call(
        pack_kernel,
        in_specs=[pl.BlockSpec(memory_space=pltpu.SMEM)] + [pl.BlockSpec(memory_space=pl.ANY)] * 4,
        out_specs=pl.BlockSpec(memory_space=pltpu.VMEM),
        out_shape=jax.ShapeDtypeStruct((inputs[0].shape[2], width), BF16),
        scratch_shapes=[pltpu.SemaphoreType.DMA((4,))],
        cost_estimate=pl.CostEstimate(flops=0, bytes_accessed=100_000, transcendentals=0),
        name="pack",
    )(side, *inputs)


def attention_kernel(scale, side_ref, *refs):
    blocks, parts = refs[:8], refs[19:25]
    q_own, g_own, k_own, v_own, q_sib, g_sib, k_sib, v_sib, own_att, own_grad, sib_out = refs[8:19]
    k_scr, v_scr, kt_scr, vt_scr, e_scr, p_scr, d_scr, q_all, c_all = refs[25:]
    slots, wide = q_own.shape[2:]
    rows = (blocks[0].shape[0] - 16) // 2
    parts = [(part, at) for part in parts for at in range(0, part.shape[0], 2 * rows)]
    prompt_len = len(blocks) * rows
    keys = [block[0:rows] for block in blocks]
    values = [block[rows : 2 * rows] for block in blocks]
    facts = [block[2 * rows :].astype(F32) for block in blocks]
    total = sum(facts[1:], facts[0])
    reward = lambda f, at: f[at + 1 : at + 2] + f[at + 2 : at + 3] + f[at + 3 : at + 4]
    reward_mean = (reward(total, 0) + reward(total, 8)) * (0.5 / len(blocks))
    keys, values = jnp.concatenate(keys, axis=0), jnp.concatenate(values, axis=0)
    keys_t, values_t = keys.T, values.T
    own = (0, q_own[0, 0], g_own[0, 0], k_own[0, 0], v_own[0, 0], own_att, own_grad)
    sib = (8, q_sib[...], g_sib[...], k_sib[...], v_sib[...], sib_out.at[:, :wide], sib_out.at[:, wide:])
    steps = []
    for n, (at, q, g, rk, rv, att, grad) in enumerate((own, sib)):
        for scr, shared, mine in ((k_scr, keys, rk), (v_scr, values, rv)):
            scr[n, :prompt_len] = shared
            scr[n, prompt_len:] = mine
        for scr, shared, mine in ((kt_scr, keys_t, rk), (vt_scr, values_t, rv)):
            scr[n, :, :prompt_len] = shared
            scr[n, :, prompt_len:] = mine.T
        cols = slice(n * (wide // HD) * slots, (n + 1) * (wide // HD) * slots)
        known = (facts[0][at : at + 1], reward(facts[0], at) - reward_mean)
        steps.append(response_steps(
            known, q, g, k_scr.at[n], v_scr.at[n], kt_scr.at[n], vt_scr.at[n], e_scr.at[n], p_scr, d_scr, q_all, c_all, cols, att, grad, scale
        ))
    a, b = steps
    turns(run(a, "S"))
    turns(run(a, "E"), run(b, "S"))
    turns(run(a, "O"), run(b, "E"))
    turns(run(a, "D"), run(b, "O"))
    turns(run(a, "G"), run(b, "D"))
    turns(run(b, "G"))
    for i, (part, at) in enumerate(parts):
        here = slice(i * rows, (i + 1) * rows)
        part[at : at + rows] = (dot(d_scr[here], q_all[...]) * scale).astype(part.dtype)
        part[at + rows : at + 2 * rows] = dot(p_scr[here], c_all[...]).astype(part.dtype)


def attention(side, blocks, resp_q, out_grad, resp_k, resp_v, packed, kv_heads):
    slots, width = resp_q.shape[2:]
    wide = width // KVH
    own = lambda w: pl.BlockSpec((1, 1, slots, w), lambda h, s: (0, 0, 0, s[0] * kv_heads + h))
    column = lambda n, w: pl.BlockSpec((n, w), lambda h, s: (0, h))
    theirs = lambda w, first: pl.BlockSpec((slots, w), lambda h, s: (0, first * kv_heads + h))
    widths = (wide, wide + 2 * HD, 2 * wide + 2 * HD)
    results = [jax.ShapeDtypeStruct((slots, kv_heads * w), BF16) for w in widths]
    height = blocks[0].shape[0] - 16
    heights = (height, height, 2 * height, 2 * height, height, height)
    parts = [jax.ShapeDtypeStruct((n, kv_heads * HD), BF16 if i else F32) for i, n in enumerate(heights)]
    keys = len(blocks) * height // 2 + slots
    rows = wide // HD * slots
    return pl.pallas_call(
        functools.partial(attention_kernel, float(HD) ** -0.5),
        grid_spec=pltpu.PrefetchScalarGridSpec(
            num_scalar_prefetch=1,
            grid=(kv_heads,),
            in_specs=[column(b.shape[0], HD) for b in blocks]
            + [own(wide), own(wide), own(HD), own(HD)]
            + [theirs(wide, 0), theirs(wide, 1), theirs(HD, 2 * wide // HD), theirs(HD, 2 * wide // HD + 1)],
            out_specs=[column(slots, w) for w in widths] + [column(n, HD) for n in heights],
            scratch_shapes=[pltpu.VMEM((2, keys, HD), BF16)] * 2
            + [pltpu.VMEM((2, HD, keys), BF16)] * 2
            + [pltpu.VMEM((2, keys, rows), F32)]
            + [pltpu.VMEM((keys, 2 * rows), BF16)] * 2
            + [pltpu.VMEM((2 * rows, HD), BF16)] * 2,
        ),
        out_shape=results + parts,
        compiler_params=pltpu.CompilerParams(vmem_limit_bytes=VMEM),
        cost_estimate=pl.CostEstimate(flops=14_000_000_000, bytes_accessed=12_000_000, transcendentals=5_000_000),
        name="attention",
    )(side, *blocks, resp_q, out_grad, resp_k, resp_v, *[packed] * 4)


def place_kernel(kv_heads, side_ref, own, sib, att):
    wide, block = att.shape[3] // kv_heads, sib.shape[1] // kv_heads
    mine = pl.program_id(0) == side_ref[0]

    @pl.when(mine)
    def _():
        att[0, 0] = own[...]

    @pl.when(jnp.logical_not(mine))
    def _():
        for h in range(kv_heads):
            att[0, 0, :, h * wide : (h + 1) * wide] = sib[:, h * block : h * block + wide]


def finish_kernel(kv_heads, count, side_ref, own, sib, total, passed, tokens, gq, gk, gv, gpk, gpv):
    wide = gq.shape[3] // kv_heads
    rows = gpk.shape[1]
    factor = count / tokens[0:1, 0:1]
    scaled = lambda values: (values.astype(F32) * factor).astype(BF16)

    def write(held):
        block = held.shape[1] // kv_heads
        for h in range(kv_heads):
            head = scaled(held[:, (h + 1) * block - wide - 2 * HD : (h + 1) * block])
            gq[0, 0, :, h * wide : (h + 1) * wide] = head[:, 0:wide]
            gk[0, 0, :, h * HD : (h + 1) * HD] = head[:, wide : wide + HD]
            gv[0, 0, :, h * HD : (h + 1) * HD] = head[:, wide + HD :]

    mine = pl.program_id(0) == side_ref[0]

    @pl.when(mine)
    def _():
        write(own)
        gpk[0] = scaled(total[0:rows])
        gpv[0] = scaled(total[2 * rows : 3 * rows])

    @pl.when(jnp.logical_not(mine))
    def _():
        write(sib)
        gpk[0] = scaled(passed[0:rows])
        gpv[0] = scaled(passed[rows:])


def halves(kernel, side, inputs, shapes, name):
    out = lambda a: pl.BlockSpec((*a.shape[:-1], a.shape[-1] // 2), lambda j, s: (0,) * (len(a.shape) - 1) + (j,))
    count = len(inputs)

    def copied(side_ref, *refs):
        sources, outs, held, sems = refs[:count], refs[count:-count - 1], refs[-count - 1 : -1], refs[-1]

        @pl.when(pl.program_id(0) == 0)
        def _():
            copies = [pltpu.make_async_copy(a, b, sems.at[i]) for i, (a, b) in enumerate(zip(sources, held))]
            for copy in copies:
                copy.start()
            for copy in copies:
                copy.wait()

        kernel(side_ref, *held, *outs)

    return pl.pallas_call(
        copied,
        grid_spec=pltpu.PrefetchScalarGridSpec(
            num_scalar_prefetch=1,
            grid=(2,),
            in_specs=[pl.BlockSpec(memory_space=pl.ANY)] * count,
            out_specs=[out(a) for a in shapes],
            scratch_shapes=[pltpu.VMEM(a.shape, a.dtype) for a in inputs] + [pltpu.SemaphoreType.DMA((count,))],
        ),
        out_shape=[jax.ShapeDtypeStruct(a.shape, BF16) for a in shapes],
        compiler_params=pltpu.CompilerParams(vmem_limit_bytes=VMEM),
        cost_estimate=pl.CostEstimate(flops=0, bytes_accessed=2_000_000, transcendentals=0),
        name=name,
    )(side, *inputs)


def body(prompt_k, prompt_v, resp_q, resp_k, resp_v, out_grad, lengths, rewards):
    slots = resp_q.shape[2]
    kv_heads = KVH // 2
    rows, width = prompt_k.shape[1:]
    pair = 2 * rows
    devices = 1
    for axis in ("x", "zh", "y", "zl", "core"):
        devices *= lax.axis_size(axis)

    keep, give, side = prep(prompt_k, prompt_v, lengths, rewards)
    got = step(give, "core", 1)
    mine = jnp.concatenate(
        [keep[:rows], got[:rows], keep[rows:pair], got[rows:pair], keep[pair : pair + 8], got[pair : pair + 8]], axis=0
    )

    tie = lax.optimization_barrier
    near_z = step(mine, "zl", 1)
    far = step(mine, "y", 2)
    below = step(mine, "y", 1)
    above = step(mine, "y", -1)
    packed = step(pack(side, resp_q, out_grad, resp_k, resp_v), "core", 1)
    near_z, packed = tie((near_z, packed))
    below_z = step(near_z, "y", 1)
    above_z = step(near_z, "y", -1)
    far_z = step(far, "zl", 1)
    blocks = (mine, near_z, above, above_z, below, below_z, far, far_z)

    tokens = sum(b[2 * pair + i : 2 * pair + i + 1, :HD].astype(F32) for b in blocks for i in (0, 8))
    tokens = jnp.broadcast_to(tokens, (8, HD))
    next_z = step(tokens, "zh", 1)
    tokens = tokens + next_z + step(tokens, "zh", -1)

    own_att, own_grad, for_sib, *parts = attention(
        side, blocks, resp_q, out_grad, resp_k, resp_v, packed, kv_heads
    )
    tokens, next_z, for_sib, *parts = tie((tokens, next_z, for_sib, *parts))
    p_own, p_near, p_above, p_below, p_far, p_far_z = parts
    height = p_far.shape[0]

    def added(*terms):
        return sum(t.astype(F32) for t in terms)

    from_z = step(p_far_z, "zl", 1)
    from_below = step(p_above, "y", 1)
    from_above = step(p_below, "y", -1)
    from_sib = step(for_sib, "core", 1)
    tokens = tokens + step(next_z, "zh", 1)
    from_z, from_below, from_above, from_sib, tokens = tie((from_z, from_below, from_above, from_sib, tokens))
    from_far = step(added(p_far, from_z).astype(BF16), "y", 2)
    from_near = step(added(p_near, from_below[height:], from_above[height:]).astype(BF16), "zl", 1)
    tokens = tokens + step(tokens, "x", 1) + step(tokens, "x", -1) + step(tokens, "x", 2)
    [attended] = halves(functools.partial(place_kernel, kv_heads), side, (own_att, from_sib), (resp_q,), "place")
    from_far, from_near, attended, tokens = tie((from_far, from_near, attended, tokens))
    total = added(p_own, from_below[:height], from_above[:height], from_far, from_near)
    pass_on = jnp.concatenate([total[rows:pair], total[pair + rows :]], axis=0).astype(BF16)
    passed = step(pass_on, "core", 1)
    grad_q, grad_rk, grad_rv, grad_pk, grad_pv = halves(
        functools.partial(finish_kernel, kv_heads, float(slots * devices)),
        side,
        (own_grad, from_sib, total, passed, tokens),
        (resp_q, resp_k, resp_v, prompt_k, prompt_v),
        "finish",
    )
    return attended, grad_q, grad_rk, grad_rv, grad_pk, grad_pv


def solution(mesh):
    parts = Mesh(mesh.devices.reshape(4, 4, 4, 2, 2), ("x", "zh", "y", "zl", "core"))
    group, member = ("x", "zh"), ("y", "zl", "core")
    rank3, rank4, rank2 = P(group, member, None), P(group, member, None, None), P(group, member)
    return jax.shard_map(
        body,
        mesh=parts,
        in_specs=(rank3, rank3, rank4, rank4, rank4, rank4, rank2, rank2),
        out_specs=(rank4, rank4, rank4, rank4, rank3, rank3),
        check_vma=False,
    )
```

```python
import functools

import jax
import jax.numpy as jnp
from jax import lax
from jax.experimental import pallas as pl
from jax.experimental.pallas import tpu as pltpu
from jax.sharding import Mesh
from jax.sharding import PartitionSpec as P

BF16 = jnp.bfloat16
F32 = jnp.float32
KVH = 8
HD = 128
S_BLOCK, BLOCK, O_BLOCK, D_BLOCK = 384, 128, 1152, 384
VMEM = 40 * 2**20
LOG2E = 1.4426950408889634
NT = (((1,), (1,)), ((), ()))
NN = (((1,), (0,)), ((), ()))


def dot(a, b, dims=NN):
    return lax.dot_general(a, b, dims, preferred_element_type=F32)


def step(values, axis, by):
    size = lax.axis_size(axis)
    return lax.ppermute(values, axis, [(i, (i + by) % size) for i in range(size)])


def swap(values, x, zh):
    rows, columns = lax.axis_size("x"), lax.axis_size("zh")
    pairs = [(i * columns + j, (i ^ x) * columns + (j ^ zh)) for i in range(rows) for j in range(columns)]
    return lax.ppermute(values, ("x", "zh"), pairs)


def heads_to_rows(wide):
    return jnp.concatenate([wide[:, i * HD : (i + 1) * HD] for i in range(wide.shape[1] // HD)], axis=0)


def tree(op, parts):
    while len(parts) > 1:
        parts = [op(*parts[i : i + 2]) if i + 1 < len(parts) else parts[i] for i in range(0, len(parts), 2)]
    return parts[0]


def response_steps(facts, queries, upstream, keys, values, keys_t, values_t, e_scr, p_scr, d_scr, q_all, c_all, cols, att, grad, scale):
    length, advantage = facts
    slots = queries.shape[0]
    key_count = e_scr.shape[0]
    prompt_len = key_count - slots
    token = lax.broadcasted_iota(jnp.int32, (slots, HD), 0).astype(F32)
    live = token < length
    weight = jnp.where(live, jnp.broadcast_to(advantage, live.shape), 0.0)
    per_head = queries.shape[1] // HD
    q_rows = heads_to_rows(queries)
    cot = [(upstream[:, i * HD : (i + 1) * HD].astype(F32) * weight).astype(BF16) for i in range(per_head)]
    cot_rows = jnp.concatenate(cot, axis=0)
    q_all[cols] = q_rows
    c_all[cols] = cot_rows
    groups = lambda a: [a[i : i + 8] for i in range(0, a.shape[0], 8)]
    tops, sums = [], []
    for first in range(0, key_count, S_BLOCK):
        scores = dot(keys[first : first + S_BLOCK], q_rows, NT)
        if first + S_BLOCK > prompt_len:
            key_pos = lax.broadcasted_iota(jnp.int32, scores.shape, 0) + (first - prompt_len)
            row_pos = lax.broadcasted_iota(jnp.int32, scores.shape, 1) % slots
            scores = jnp.where(key_pos <= row_pos, scores, -jnp.inf)
        e_scr[first : first + S_BLOCK] = scores
        tops.append(tree(jnp.maximum, groups(scores)))
        yield
    yield "S"
    row_max = jnp.max(tree(jnp.maximum, tops), axis=0, keepdims=True) * (scale * LOG2E)
    for first in range(0, key_count, BLOCK):
        raised = jnp.exp2(e_scr[first : first + BLOCK] * (scale * LOG2E) - row_max)
        e_scr[first : first + BLOCK] = raised
        sums.append(tree(jnp.add, groups(raised)))
        yield
    yield "E"
    inverse = 1.0 / jnp.sum(tree(jnp.add, sums), axis=0, keepdims=True)
    output_t = None
    for first in range(0, key_count, O_BLOCK):
        for at in range(first, first + O_BLOCK, BLOCK):
            p_scr[at : at + BLOCK, cols] = (e_scr[at : at + BLOCK] * inverse).astype(BF16)
        term = dot(values_t[:, first : first + O_BLOCK], p_scr[first : first + O_BLOCK, cols])
        output_t = term if output_t is None else output_t + term
        yield
    yield "O"
    cot_t = cot_rows.astype(F32).T
    delta = jnp.sum(cot_t * output_t, axis=0, keepdims=True)
    for i in range(per_head):
        att[:, i * HD : (i + 1) * HD] = jnp.where(live, output_t[:, i * slots : (i + 1) * slots].T, 0.0).astype(BF16)
    for first in range(0, key_count, D_BLOCK):
        dprobs = dot(values[first : first + D_BLOCK], cot_rows, NT)
        probs = e_scr[first : first + D_BLOCK] * inverse
        d_scr[first : first + D_BLOCK, cols] = (probs * (dprobs - delta)).astype(BF16)
        yield
    yield "D"
    grad_q_t = dot(keys_t[...], d_scr[:, cols]) * scale
    for i in range(per_head):
        grad[:, i * HD : (i + 1) * HD] = grad_q_t[:, i * slots : (i + 1) * slots].T.astype(BF16)
    wide = per_head * HD
    grad[:, wide : wide + HD] = (dot(d_scr[prompt_len:, cols], q_rows) * scale).astype(BF16)
    grad[:, wide + HD :] = dot(p_scr[prompt_len:, cols], cot_rows).astype(BF16)
    yield "G"


def run(steps, until):
    for mark in steps:
        yield
        if mark == until:
            return


def turns(*runs):
    runs = list(runs)
    while runs:
        for r in list(runs):
            try:
                next(r)
            except StopIteration:
                runs.remove(r)


def prep_kernel(k_in, v_in, length_in, reward_in, keep, give, side_out):
    rows, width = k_in.shape[1:]
    half = width // 2
    reward = jnp.broadcast_to(reward_in[...], (16, half))
    length = jnp.broadcast_to(length_in[...].astype(F32), (16, half))
    high = reward.astype(BF16).astype(F32)
    middle = (reward - high).astype(BF16).astype(F32)
    row = lax.broadcasted_iota(jnp.int32, (16, half), 0) % 8
    facts = length
    for at, value in ((1, high), (2, middle), (3, reward - high - middle)):
        facts = jnp.where(row == at, value, facts)
    facts = jnp.where(row < 4, facts, 0.0).astype(BF16)

    def write(mine, other):
        for out, cols in ((mine, slice(0, half)), (other, slice(half, width))):
            out[0:rows] = k_in[0, :, cols]
            out[rows : 2 * rows] = v_in[0, :, cols]
            out[2 * rows :] = facts

    side = lax.axis_index("core")
    side_out[0] = side.astype(jnp.int32)
    pl.when(side == 0)(lambda: write(keep, give))
    pl.when(side != 0)(lambda: write(give, keep))


def prep(prompt_k, prompt_v, lengths, rewards):
    _, rows, width = prompt_k.shape
    whole = lambda shape: pl.BlockSpec(shape, lambda i: (0,) * len(shape))
    out = jax.ShapeDtypeStruct((2 * rows + 16, width // 2), BF16)
    return pl.pallas_call(
        prep_kernel,
        grid=(1,),
        in_specs=[whole(a.shape) for a in (prompt_k, prompt_v, lengths, rewards)],
        out_specs=[whole(out.shape), whole(out.shape), pl.BlockSpec(memory_space=pltpu.SMEM)],
        out_shape=[out, out, jax.ShapeDtypeStruct((1,), jnp.int32)],
        cost_estimate=pl.CostEstimate(flops=0, bytes_accessed=500_000, transcendentals=0),
        name="prep",
    )(prompt_k, prompt_v, lengths, rewards)


def pack_kernel(side_ref, *refs):
    inputs, out, sems = refs[:4], refs[4], refs[5]
    other = 1 - side_ref[0]
    copies, first = [], 0
    for i, a in enumerate(inputs):
        half = a.shape[3] // 2
        source = a.at[0, 0, :, pl.ds(pl.multiple_of(other * half, HD), half)]
        copies.append(pltpu.make_async_copy(source, out.at[:, first : first + half], sems.at[i]))
        first += half
    for copy in copies:
        copy.start()
    for copy in copies:
        copy.wait()


def pack(side, *inputs):
    width = sum(a.shape[3] for a in inputs) // 2
    return pl.pallas_call(
        pack_kernel,
        in_specs=[pl.BlockSpec(memory_space=pltpu.SMEM)] + [pl.BlockSpec(memory_space=pl.ANY)] * 4,
        out_specs=pl.BlockSpec(memory_space=pltpu.VMEM),
        out_shape=jax.ShapeDtypeStruct((inputs[0].shape[2], width), BF16),
        scratch_shapes=[pltpu.SemaphoreType.DMA((4,))],
        cost_estimate=pl.CostEstimate(flops=0, bytes_accessed=100_000, transcendentals=0),
        name="pack",
    )(side, *inputs)


def attention_kernel(scale, side_ref, *refs):
    blocks, parts = refs[:8], refs[19:27]
    q_own, g_own, k_own, v_own, q_sib, g_sib, k_sib, v_sib, own_att, own_grad, sib_out = refs[8:19]
    k_scr, v_scr, kt_scr, vt_scr, e_scr, p_scr, d_scr, q_all, c_all = refs[27:]
    slots, wide = q_own.shape[2:]
    rows = (blocks[0].shape[0] - 16) // 2
    prompt_len = len(blocks) * rows
    keys = [block[0:rows] for block in blocks]
    values = [block[rows : 2 * rows] for block in blocks]
    facts = [block[2 * rows :].astype(F32) for block in blocks]
    total = sum(facts[1:], facts[0])
    reward = lambda f, at: f[at + 1 : at + 2] + f[at + 2 : at + 3] + f[at + 3 : at + 4]
    reward_mean = (reward(total, 0) + reward(total, 8)) * (0.5 / len(blocks))
    keys, values = jnp.concatenate(keys, axis=0), jnp.concatenate(values, axis=0)
    keys_t, values_t = keys.T, values.T
    own = (0, q_own[0, 0], g_own[0, 0], k_own[0, 0], v_own[0, 0], own_att, own_grad)
    sib = (8, q_sib[...], g_sib[...], k_sib[...], v_sib[...], sib_out.at[:, :wide], sib_out.at[:, wide:])
    steps = []
    for n, (at, q, g, rk, rv, att, grad) in enumerate((own, sib)):
        for scr, shared, mine in ((k_scr, keys, rk), (v_scr, values, rv)):
            scr[n, :prompt_len] = shared
            scr[n, prompt_len:] = mine
        for scr, shared, mine in ((kt_scr, keys_t, rk), (vt_scr, values_t, rv)):
            scr[n, :, :prompt_len] = shared
            scr[n, :, prompt_len:] = mine.T
        cols = slice(n * (wide // HD) * slots, (n + 1) * (wide // HD) * slots)
        known = (facts[0][at : at + 1], reward(facts[0], at) - reward_mean)
        steps.append(response_steps(
            known, q, g, k_scr.at[n], v_scr.at[n], kt_scr.at[n], vt_scr.at[n], e_scr.at[n], p_scr, d_scr, q_all, c_all, cols, att, grad, scale
        ))
    a, b = steps
    turns(run(a, "S"))
    turns(run(a, "E"), run(b, "S"))
    turns(run(a, "O"), run(b, "E"))
    turns(run(a, "D"), run(b, "O"))
    turns(run(a, "G"), run(b, "D"))
    turns(run(b, "G"))
    for i, part in enumerate(parts):
        here = slice(i * rows, (i + 1) * rows)
        part[0:rows] = (dot(d_scr[here], q_all[...]) * scale).astype(part.dtype)
        part[rows:] = dot(p_scr[here], c_all[...]).astype(part.dtype)


def attention(side, blocks, resp_q, out_grad, resp_k, resp_v, packed, kv_heads):
    slots, width = resp_q.shape[2:]
    wide = width // KVH
    own = lambda w: pl.BlockSpec((1, 1, slots, w), lambda h, s: (0, 0, 0, s[0] * kv_heads + h))
    column = lambda n, w: pl.BlockSpec((n, w), lambda h, s: (0, h))
    theirs = lambda w, first: pl.BlockSpec((slots, w), lambda h, s: (0, first * kv_heads + h))
    widths = (wide, wide + 2 * HD, 2 * wide + 2 * HD)
    results = [jax.ShapeDtypeStruct((slots, kv_heads * w), BF16) for w in widths]
    height = blocks[0].shape[0] - 16
    parts = [jax.ShapeDtypeStruct((height, kv_heads * HD), BF16 if i else F32) for i in range(len(blocks))]
    keys = len(blocks) * height // 2 + slots
    rows = wide // HD * slots
    return pl.pallas_call(
        functools.partial(attention_kernel, float(HD) ** -0.5),
        grid_spec=pltpu.PrefetchScalarGridSpec(
            num_scalar_prefetch=1,
            grid=(kv_heads,),
            in_specs=[column(b.shape[0], HD) for b in blocks]
            + [own(wide), own(wide), own(HD), own(HD)]
            + [theirs(wide, 0), theirs(wide, 1), theirs(HD, 2 * wide // HD), theirs(HD, 2 * wide // HD + 1)],
            out_specs=[column(slots, w) for w in widths] + [column(height, HD)] * len(parts),
            scratch_shapes=[pltpu.VMEM((2, keys, HD), BF16)] * 2
            + [pltpu.VMEM((2, HD, keys), BF16)] * 2
            + [pltpu.VMEM((2, keys, rows), F32)]
            + [pltpu.VMEM((keys, 2 * rows), BF16)] * 2
            + [pltpu.VMEM((2 * rows, HD), BF16)] * 2,
        ),
        out_shape=results + parts,
        compiler_params=pltpu.CompilerParams(vmem_limit_bytes=VMEM),
        cost_estimate=pl.CostEstimate(flops=14_000_000_000, bytes_accessed=12_000_000, transcendentals=5_000_000),
        name="attention",
    )(side, *blocks, resp_q, out_grad, resp_k, resp_v, *[packed] * 4)


def place_kernel(kv_heads, side_ref, own, sib, att):
    wide, block = att.shape[3] // kv_heads, sib.shape[1] // kv_heads
    mine = pl.program_id(0) == side_ref[0]

    @pl.when(mine)
    def _():
        att[0, 0] = own[...]

    @pl.when(jnp.logical_not(mine))
    def _():
        for h in range(kv_heads):
            att[0, 0, :, h * wide : (h + 1) * wide] = sib[:, h * block : h * block + wide]


def finish_kernel(kv_heads, count, side_ref, own, sib, total, passed, tokens, gq, gk, gv, gpk, gpv):
    wide = gq.shape[3] // kv_heads
    rows = gpk.shape[1]
    factor = count / tokens[0:1, 0:1]
    scaled = lambda values: (values.astype(F32) * factor).astype(BF16)

    def write(held):
        block = held.shape[1] // kv_heads
        for h in range(kv_heads):
            head = scaled(held[:, (h + 1) * block - wide - 2 * HD : (h + 1) * block])
            gq[0, 0, :, h * wide : (h + 1) * wide] = head[:, 0:wide]
            gk[0, 0, :, h * HD : (h + 1) * HD] = head[:, wide : wide + HD]
            gv[0, 0, :, h * HD : (h + 1) * HD] = head[:, wide + HD :]

    mine = pl.program_id(0) == side_ref[0]

    @pl.when(mine)
    def _():
        write(own)
        gpk[0] = scaled(total[0:rows])
        gpv[0] = scaled(total[2 * rows : 3 * rows])

    @pl.when(jnp.logical_not(mine))
    def _():
        write(sib)
        gpk[0] = scaled(passed[0:rows])
        gpv[0] = scaled(passed[rows:])


def halves(kernel, side, inputs, shapes, name):
    out = lambda a: pl.BlockSpec((*a.shape[:-1], a.shape[-1] // 2), lambda j, s: (0,) * (len(a.shape) - 1) + (j,))
    count = len(inputs)

    def copied(side_ref, *refs):
        sources, outs, held, sems = refs[:count], refs[count:-count - 1], refs[-count - 1 : -1], refs[-1]

        @pl.when(pl.program_id(0) == 0)
        def _():
            copies = [pltpu.make_async_copy(a, b, sems.at[i]) for i, (a, b) in enumerate(zip(sources, held))]
            for copy in copies:
                copy.start()
            for copy in copies:
                copy.wait()

        kernel(side_ref, *held, *outs)

    return pl.pallas_call(
        copied,
        grid_spec=pltpu.PrefetchScalarGridSpec(
            num_scalar_prefetch=1,
            grid=(2,),
            in_specs=[pl.BlockSpec(memory_space=pl.ANY)] * count,
            out_specs=[out(a) for a in shapes],
            scratch_shapes=[pltpu.VMEM(a.shape, a.dtype) for a in inputs] + [pltpu.SemaphoreType.DMA((count,))],
        ),
        out_shape=[jax.ShapeDtypeStruct(a.shape, BF16) for a in shapes],
        compiler_params=pltpu.CompilerParams(vmem_limit_bytes=VMEM),
        cost_estimate=pl.CostEstimate(flops=0, bytes_accessed=2_000_000, transcendentals=0),
        name=name,
    )(side, *inputs)


def body(prompt_k, prompt_v, resp_q, resp_k, resp_v, out_grad, lengths, rewards):
    slots = resp_q.shape[2]
    kv_heads = KVH // 2
    rows, width = prompt_k.shape[1:]
    pair = 2 * rows
    devices = 1
    for axis in ("x", "zh", "y", "zl", "core"):
        devices *= lax.axis_size(axis)

    keep, give, side = prep(prompt_k, prompt_v, lengths, rewards)
    got = step(give, "core", 1)
    mine = jnp.concatenate(
        [keep[:rows], got[:rows], keep[rows:pair], got[rows:pair], keep[pair : pair + 8], got[pair : pair + 8]], axis=0
    )

    tie = lax.optimization_barrier
    near_z = step(mine, "zl", 1)
    far = step(mine, "y", 2)
    below = step(mine, "y", 1)
    above = step(mine, "y", -1)
    packed = step(pack(side, resp_q, out_grad, resp_k, resp_v), "core", 1)
    near_z, packed = tie((near_z, packed))
    below_z = step(near_z, "y", 1)
    above_z = step(near_z, "y", -1)
    far_z = step(far, "zl", 1)
    blocks = (mine, near_z, above, above_z, below, below_z, far, far_z)

    tokens = sum(b[2 * pair + i : 2 * pair + i + 1, :HD].astype(F32) for b in blocks for i in (0, 8))
    tokens = jnp.broadcast_to(tokens, (8, HD))
    tokens = tokens + swap(tokens, 1, 0) + swap(tokens, 0, 1) + swap(tokens, 1, 1)

    own_att, own_grad, for_sib, *parts = attention(
        side, blocks, resp_q, out_grad, resp_k, resp_v, packed, kv_heads
    )
    tokens, for_sib, *parts = tie((tokens, for_sib, *parts))
    p_own, p_near, p_above, p_above_z, p_below, p_below_z, p_far, p_far_z = parts

    def added(*terms):
        return sum(t.astype(F32) for t in terms)

    from_z = step(p_far_z, "zl", 1)
    from_below_z = step(p_above_z, "y", 1)
    from_above_z = step(p_below_z, "y", -1)
    from_sib = step(for_sib, "core", 1)
    tokens = tokens + swap(tokens, 3, 0)
    from_z, from_below_z, from_above_z, from_sib, tokens, p_above, p_below = tie(
        (from_z, from_below_z, from_above_z, from_sib, tokens, p_above, p_below)
    )
    from_below = step(p_above, "y", 1)
    from_above = step(p_below, "y", -1)
    from_far = step(added(p_far, from_z).astype(BF16), "y", 2)
    from_near = step(added(p_near, from_below_z, from_above_z).astype(BF16), "zl", 1)
    tokens = tokens + swap(tokens, 0, 3)
    [attended] = halves(functools.partial(place_kernel, kv_heads), side, (own_att, from_sib), (resp_q,), "place")
    from_far, from_near, from_below, from_above, attended, tokens = tie(
        (from_far, from_near, from_below, from_above, attended, tokens)
    )
    total = added(p_own, from_below, from_above, from_far, from_near)
    pass_on = jnp.concatenate([total[rows:pair], total[pair + rows :]], axis=0).astype(BF16)
    passed = step(pass_on, "core", 1)
    grad_q, grad_rk, grad_rv, grad_pk, grad_pv = halves(
        functools.partial(finish_kernel, kv_heads, float(slots * devices)),
        side,
        (own_grad, from_sib, total, passed, tokens),
        (resp_q, resp_k, resp_v, prompt_k, prompt_v),
        "finish",
    )
    return attended, grad_q, grad_rk, grad_rv, grad_pk, grad_pv


def solution(mesh):
    parts = Mesh(mesh.devices.reshape(4, 4, 4, 2, 2), ("x", "zh", "y", "zl", "core"))
    group, member = ("x", "zh"), ("y", "zl", "core")
    rank3, rank4, rank2 = P(group, member, None), P(group, member, None, None), P(group, member)
    return jax.shard_map(
        body,
        mesh=parts,
        in_specs=(rank3, rank3, rank4, rank4, rank4, rank4, rank2, rank2),
        out_specs=(rank4, rank4, rank4, rank4, rank3, rank3),
        check_vma=False,
    )
```

```python
import functools

import jax
import jax.numpy as jnp
from jax import lax
from jax.experimental import pallas as pl
from jax.experimental.pallas import tpu as pltpu
from jax.sharding import Mesh
from jax.sharding import PartitionSpec as P

BF16 = jnp.bfloat16
F32 = jnp.float32
KVH = 8
HD = 128
S_BLOCK, BLOCK, O_BLOCK, D_BLOCK = 384, 128, 1152, 384
VMEM = 40 * 2**20
LOG2E = 1.4426950408889634
NT = (((1,), (1,)), ((), ()))
NN = (((1,), (0,)), ((), ()))


def dot(a, b, dims=NN):
    return lax.dot_general(a, b, dims, preferred_element_type=F32)


def step(values, axis, by):
    size = lax.axis_size(axis)
    return lax.ppermute(values, axis, [(i, (i + by) % size) for i in range(size)])


def swap(values, x, zh):
    rows, columns = lax.axis_size("x"), lax.axis_size("zh")
    pairs = [(i * columns + j, (i ^ x) * columns + (j ^ zh)) for i in range(rows) for j in range(columns)]
    return lax.ppermute(values, ("x", "zh"), pairs)


def heads_to_rows(wide):
    return jnp.concatenate([wide[:, i * HD : (i + 1) * HD] for i in range(wide.shape[1] // HD)], axis=0)


def tree(op, parts):
    while len(parts) > 1:
        parts = [op(*parts[i : i + 2]) if i + 1 < len(parts) else parts[i] for i in range(0, len(parts), 2)]
    return parts[0]


def response_steps(facts, queries, upstream, keys, values, keys_t, values_t, e_scr, p_scr, d_scr, q_all, c_all, cols, att, grad, scale):
    length, advantage = facts
    slots = queries.shape[0]
    key_count = e_scr.shape[0]
    prompt_len = key_count - slots
    token = lax.broadcasted_iota(jnp.int32, (slots, HD), 0).astype(F32)
    live = token < length
    weight = jnp.where(live, jnp.broadcast_to(advantage, live.shape), 0.0)
    per_head = queries.shape[1] // HD
    q_rows = heads_to_rows(queries)
    cot = [(upstream[:, i * HD : (i + 1) * HD].astype(F32) * weight).astype(BF16) for i in range(per_head)]
    cot_rows = jnp.concatenate(cot, axis=0)
    q_all[cols] = q_rows
    c_all[cols] = cot_rows
    groups = lambda a: [a[i : i + 8] for i in range(0, a.shape[0], 8)]
    tops, sums = [], []
    for first in range(0, key_count, S_BLOCK):
        scores = dot(keys[first : first + S_BLOCK], q_rows, NT)
        if first + S_BLOCK > prompt_len:
            key_pos = lax.broadcasted_iota(jnp.int32, scores.shape, 0) + (first - prompt_len)
            row_pos = lax.broadcasted_iota(jnp.int32, scores.shape, 1) % slots
            scores = jnp.where(key_pos <= row_pos, scores, -jnp.inf)
        e_scr[first : first + S_BLOCK] = scores
        tops.append(tree(jnp.maximum, groups(scores)))
        yield
    yield "S"
    row_max = jnp.max(tree(jnp.maximum, tops), axis=0, keepdims=True) * (scale * LOG2E)
    for first in range(0, key_count, BLOCK):
        raised = jnp.exp2(e_scr[first : first + BLOCK] * (scale * LOG2E) - row_max)
        e_scr[first : first + BLOCK] = raised
        sums.append(tree(jnp.add, groups(raised)))
        yield
    yield "E"
    inverse = 1.0 / jnp.sum(tree(jnp.add, sums), axis=0, keepdims=True)
    output_t = None
    for first in range(0, key_count, O_BLOCK):
        for at in range(first, first + O_BLOCK, BLOCK):
            p_scr[at : at + BLOCK, cols] = (e_scr[at : at + BLOCK] * inverse).astype(BF16)
        term = dot(values_t[:, first : first + O_BLOCK], p_scr[first : first + O_BLOCK, cols])
        output_t = term if output_t is None else output_t + term
        yield
    yield "O"
    cot_t = cot_rows.astype(F32).T
    delta = jnp.sum(cot_t * output_t, axis=0, keepdims=True)
    for i in range(per_head):
        att[:, i * HD : (i + 1) * HD] = jnp.where(live, output_t[:, i * slots : (i + 1) * slots].T, 0.0).astype(BF16)
    for first in range(0, key_count, D_BLOCK):
        dprobs = dot(values[first : first + D_BLOCK], cot_rows, NT)
        probs = e_scr[first : first + D_BLOCK] * inverse
        d_scr[first : first + D_BLOCK, cols] = (probs * (dprobs - delta)).astype(BF16)
        yield
    yield "D"
    grad_q_t = dot(keys_t[...], d_scr[:, cols]) * scale
    for i in range(per_head):
        grad[:, i * HD : (i + 1) * HD] = grad_q_t[:, i * slots : (i + 1) * slots].T.astype(BF16)
    wide = per_head * HD
    grad[:, wide : wide + HD] = (dot(d_scr[prompt_len:, cols], q_rows) * scale).astype(BF16)
    grad[:, wide + HD :] = dot(p_scr[prompt_len:, cols], cot_rows).astype(BF16)
    yield "G"


def run(steps, until):
    for mark in steps:
        yield
        if mark == until:
            return


def turns(*runs):
    runs = list(runs)
    while runs:
        for r in list(runs):
            try:
                next(r)
            except StopIteration:
                runs.remove(r)


def prep_kernel(k_in, v_in, length_in, reward_in, keep, give, side_out):
    rows, width = k_in.shape[1:]
    half = width // 2
    reward = jnp.broadcast_to(reward_in[...], (16, half))
    length = jnp.broadcast_to(length_in[...].astype(F32), (16, half))
    high = reward.astype(BF16).astype(F32)
    middle = (reward - high).astype(BF16).astype(F32)
    row = lax.broadcasted_iota(jnp.int32, (16, half), 0) % 8
    facts = length
    for at, value in ((1, high), (2, middle), (3, reward - high - middle)):
        facts = jnp.where(row == at, value, facts)
    facts = jnp.where(row < 4, facts, 0.0).astype(BF16)

    def write(mine, other):
        for out, cols in ((mine, slice(0, half)), (other, slice(half, width))):
            out[0:rows] = k_in[0, :, cols]
            out[rows : 2 * rows] = v_in[0, :, cols]
            out[2 * rows :] = facts

    side = lax.axis_index("core")
    side_out[0] = side.astype(jnp.int32)
    pl.when(side == 0)(lambda: write(keep, give))
    pl.when(side != 0)(lambda: write(give, keep))


def prep(prompt_k, prompt_v, lengths, rewards):
    _, rows, width = prompt_k.shape
    whole = lambda shape: pl.BlockSpec(shape, lambda i: (0,) * len(shape))
    out = jax.ShapeDtypeStruct((2 * rows + 16, width // 2), BF16)
    return pl.pallas_call(
        prep_kernel,
        grid=(1,),
        in_specs=[whole(a.shape) for a in (prompt_k, prompt_v, lengths, rewards)],
        out_specs=[whole(out.shape), whole(out.shape), pl.BlockSpec(memory_space=pltpu.SMEM)],
        out_shape=[out, out, jax.ShapeDtypeStruct((1,), jnp.int32)],
        cost_estimate=pl.CostEstimate(flops=0, bytes_accessed=500_000, transcendentals=0),
        name="prep",
    )(prompt_k, prompt_v, lengths, rewards)


def pack_kernel(side_ref, *refs):
    inputs, out, sems = refs[:4], refs[4], refs[5]
    other = 1 - side_ref[0]
    copies, first = [], 0
    for i, a in enumerate(inputs):
        half = a.shape[3] // 2
        source = a.at[0, 0, :, pl.ds(pl.multiple_of(other * half, HD), half)]
        copies.append(pltpu.make_async_copy(source, out.at[:, first : first + half], sems.at[i]))
        first += half
    for copy in copies:
        copy.start()
    for copy in copies:
        copy.wait()


def pack(side, *inputs):
    width = sum(a.shape[3] for a in inputs) // 2
    return pl.pallas_call(
        pack_kernel,
        in_specs=[pl.BlockSpec(memory_space=pltpu.SMEM)] + [pl.BlockSpec(memory_space=pl.ANY)] * 4,
        out_specs=pl.BlockSpec(memory_space=pltpu.VMEM),
        out_shape=jax.ShapeDtypeStruct((inputs[0].shape[2], width), BF16),
        scratch_shapes=[pltpu.SemaphoreType.DMA((4,))],
        cost_estimate=pl.CostEstimate(flops=0, bytes_accessed=100_000, transcendentals=0),
        name="pack",
    )(side, *inputs)


def attention_kernel(scale, side_ref, *refs):
    blocks, parts = refs[:8], refs[19:27]
    q_own, g_own, k_own, v_own, q_sib, g_sib, k_sib, v_sib, own_att, own_grad, sib_out = refs[8:19]
    k_scr, v_scr, kt_scr, vt_scr, e_scr, p_scr, d_scr, q_all, c_all = refs[27:]
    slots, wide = q_own.shape[2:]
    rows = (blocks[0].shape[0] - 16) // 2
    prompt_len = len(blocks) * rows
    keys = [block[0:rows] for block in blocks]
    values = [block[rows : 2 * rows] for block in blocks]
    facts = [block[2 * rows :].astype(F32) for block in blocks]
    total = sum(facts[1:], facts[0])
    reward = lambda f, at: f[at + 1 : at + 2] + f[at + 2 : at + 3] + f[at + 3 : at + 4]
    reward_mean = (reward(total, 0) + reward(total, 8)) * (0.5 / len(blocks))
    keys, values = jnp.concatenate(keys, axis=0), jnp.concatenate(values, axis=0)
    keys_t, values_t = keys.T, values.T
    own = (0, q_own[0, 0], g_own[0, 0], k_own[0, 0], v_own[0, 0], own_att, own_grad)
    sib = (8, q_sib[...], g_sib[...], k_sib[...], v_sib[...], sib_out.at[:, :wide], sib_out.at[:, wide:])
    steps = []
    for n, (at, q, g, rk, rv, att, grad) in enumerate((own, sib)):
        for scr, shared, mine in ((k_scr, keys, rk), (v_scr, values, rv)):
            scr[n, :prompt_len] = shared
            scr[n, prompt_len:] = mine
        for scr, shared, mine in ((kt_scr, keys_t, rk), (vt_scr, values_t, rv)):
            scr[n, :, :prompt_len] = shared
            scr[n, :, prompt_len:] = mine.T
        cols = slice(n * (wide // HD) * slots, (n + 1) * (wide // HD) * slots)
        known = (facts[0][at : at + 1], reward(facts[0], at) - reward_mean)
        steps.append(response_steps(
            known, q, g, k_scr.at[n], v_scr.at[n], kt_scr.at[n], vt_scr.at[n], e_scr.at[n], p_scr, d_scr, q_all, c_all, cols, att, grad, scale
        ))
    a, b = steps
    turns(run(a, "S"))
    turns(run(a, "E"), run(b, "S"))
    turns(run(a, "O"), run(b, "E"))
    turns(run(a, "D"), run(b, "O"))
    turns(run(a, "G"), run(b, "D"))
    turns(run(b, "G"))
    for i, part in enumerate(parts):
        here = slice(i * rows, (i + 1) * rows)
        part[0:rows] = (dot(d_scr[here], q_all[...]) * scale).astype(part.dtype)
        part[rows:] = dot(p_scr[here], c_all[...]).astype(part.dtype)


def attention(side, blocks, resp_q, out_grad, resp_k, resp_v, packed, kv_heads):
    slots, width = resp_q.shape[2:]
    wide = width // KVH
    own = lambda w: pl.BlockSpec((1, 1, slots, w), lambda h, s: (0, 0, 0, s[0] * kv_heads + h))
    column = lambda n, w: pl.BlockSpec((n, w), lambda h, s: (0, h))
    theirs = lambda w, first: pl.BlockSpec((slots, w), lambda h, s: (0, first * kv_heads + h))
    widths = (wide, wide + 2 * HD, 2 * wide + 2 * HD)
    results = [jax.ShapeDtypeStruct((slots, kv_heads * w), BF16) for w in widths]
    height = blocks[0].shape[0] - 16
    parts = [jax.ShapeDtypeStruct((height, kv_heads * HD), BF16 if i else F32) for i in range(len(blocks))]
    keys = len(blocks) * height // 2 + slots
    rows = wide // HD * slots
    return pl.pallas_call(
        functools.partial(attention_kernel, float(HD) ** -0.5),
        grid_spec=pltpu.PrefetchScalarGridSpec(
            num_scalar_prefetch=1,
            grid=(kv_heads,),
            in_specs=[column(b.shape[0], HD) for b in blocks]
            + [own(wide), own(wide), own(HD), own(HD)]
            + [theirs(wide, 0), theirs(wide, 1), theirs(HD, 2 * wide // HD), theirs(HD, 2 * wide // HD + 1)],
            out_specs=[column(slots, w) for w in widths] + [column(height, HD)] * len(parts),
            scratch_shapes=[pltpu.VMEM((2, keys, HD), BF16)] * 2
            + [pltpu.VMEM((2, HD, keys), BF16)] * 2
            + [pltpu.VMEM((2, keys, rows), F32)]
            + [pltpu.VMEM((keys, 2 * rows), BF16)] * 2
            + [pltpu.VMEM((2 * rows, HD), BF16)] * 2,
        ),
        out_shape=results + parts,
        compiler_params=pltpu.CompilerParams(vmem_limit_bytes=VMEM),
        cost_estimate=pl.CostEstimate(flops=14_000_000_000, bytes_accessed=12_000_000, transcendentals=5_000_000),
        name="attention",
    )(side, *blocks, resp_q, out_grad, resp_k, resp_v, *[packed] * 4)


def place_kernel(kv_heads, side_ref, own, sib, att):
    wide, block = att.shape[3] // kv_heads, sib.shape[1] // kv_heads
    mine = pl.program_id(0) == side_ref[0]

    @pl.when(mine)
    def _():
        att[0, 0] = own[...]

    @pl.when(jnp.logical_not(mine))
    def _():
        for h in range(kv_heads):
            att[0, 0, :, h * wide : (h + 1) * wide] = sib[:, h * block : h * block + wide]


def finish_kernel(kv_heads, count, side_ref, own, sib, total, passed, tokens, gq, gk, gv, gpk, gpv):
    wide = gq.shape[3] // kv_heads
    rows = gpk.shape[1]
    factor = count / tokens[0:1, 0:1]
    scaled = lambda values: (values.astype(F32) * factor).astype(BF16)

    def write(held):
        block = held.shape[1] // kv_heads
        for h in range(kv_heads):
            head = scaled(held[:, (h + 1) * block - wide - 2 * HD : (h + 1) * block])
            gq[0, 0, :, h * wide : (h + 1) * wide] = head[:, 0:wide]
            gk[0, 0, :, h * HD : (h + 1) * HD] = head[:, wide : wide + HD]
            gv[0, 0, :, h * HD : (h + 1) * HD] = head[:, wide + HD :]

    mine = pl.program_id(0) == side_ref[0]

    @pl.when(mine)
    def _():
        write(own)
        gpk[0] = scaled(total[0:rows])
        gpv[0] = scaled(total[2 * rows : 3 * rows])

    @pl.when(jnp.logical_not(mine))
    def _():
        write(sib)
        gpk[0] = scaled(passed[0:rows])
        gpv[0] = scaled(passed[rows:])


def halves(kernel, side, inputs, shapes, name):
    out = lambda a: pl.BlockSpec((*a.shape[:-1], a.shape[-1] // 2), lambda j, s: (0,) * (len(a.shape) - 1) + (j,))
    count = len(inputs)

    def copied(side_ref, *refs):
        sources, outs, held, sems = refs[:count], refs[count:-count - 1], refs[-count - 1 : -1], refs[-1]

        @pl.when(pl.program_id(0) == 0)
        def _():
            copies = [pltpu.make_async_copy(a, b, sems.at[i]) for i, (a, b) in enumerate(zip(sources, held))]
            for copy in copies:
                copy.start()
            for copy in copies:
                copy.wait()

        kernel(side_ref, *held, *outs)

    return pl.pallas_call(
        copied,
        grid_spec=pltpu.PrefetchScalarGridSpec(
            num_scalar_prefetch=1,
            grid=(2,),
            in_specs=[pl.BlockSpec(memory_space=pl.ANY)] * count,
            out_specs=[out(a) for a in shapes],
            scratch_shapes=[pltpu.VMEM(a.shape, a.dtype) for a in inputs] + [pltpu.SemaphoreType.DMA((count,))],
        ),
        out_shape=[jax.ShapeDtypeStruct(a.shape, BF16) for a in shapes],
        compiler_params=pltpu.CompilerParams(vmem_limit_bytes=VMEM),
        cost_estimate=pl.CostEstimate(flops=0, bytes_accessed=2_000_000, transcendentals=0),
        name=name,
    )(side, *inputs)


def body(prompt_k, prompt_v, resp_q, resp_k, resp_v, out_grad, lengths, rewards):
    slots = resp_q.shape[2]
    kv_heads = KVH // 2
    rows, width = prompt_k.shape[1:]
    pair = 2 * rows
    devices = 1
    for axis in ("x", "zh", "y", "zl", "core"):
        devices *= lax.axis_size(axis)

    keep, give, side = prep(prompt_k, prompt_v, lengths, rewards)
    got = step(give, "core", 1)
    mine = jnp.concatenate(
        [keep[:rows], got[:rows], keep[rows:pair], got[rows:pair], keep[pair : pair + 8], got[pair : pair + 8]], axis=0
    )

    tie = lax.optimization_barrier
    near_z = step(mine, "zl", 1)
    far = step(mine, "y", 2)
    below = step(mine, "y", 1)
    above = step(mine, "y", -1)
    packed = step(pack(side, resp_q, out_grad, resp_k, resp_v), "core", 1)
    near_z, packed = tie((near_z, packed))
    below_z = step(near_z, "y", 1)
    above_z = step(near_z, "y", -1)
    far_z = step(far, "zl", 1)
    blocks = (mine, near_z, above, above_z, below, below_z, far, far_z)

    tokens = sum(b[2 * pair + i : 2 * pair + i + 1, :HD].astype(F32) for b in (mine, above, below, far) for i in (0, 8))
    tokens = jnp.broadcast_to(tokens, (8, HD))
    tokens = tokens + swap(tokens, 1, 0) + swap(tokens, 0, 1) + swap(tokens, 1, 1)
    below_z, above_z, far_z, tokens = tie((below_z, above_z, far_z, tokens))
    blocks = (mine, near_z, above, above_z, below, below_z, far, far_z)
    tokens = tokens + step(tokens, "zl", 1)

    own_att, own_grad, for_sib, *parts = attention(
        side, blocks, resp_q, out_grad, resp_k, resp_v, packed, kv_heads
    )
    tokens, for_sib, *parts = tie((tokens, for_sib, *parts))
    p_own, p_near, p_above, p_above_z, p_below, p_below_z, p_far, p_far_z = parts

    def added(*terms):
        return sum(t.astype(F32) for t in terms)

    from_z = step(p_far_z, "zl", 1)
    from_below_z = step(p_above_z, "y", 1)
    from_above_z = step(p_below_z, "y", -1)
    from_sib = step(for_sib, "core", 1)
    tokens = tokens + swap(tokens, 3, 0)
    from_z, from_below_z, from_above_z, from_sib, tokens, p_above, p_below = tie(
        (from_z, from_below_z, from_above_z, from_sib, tokens, p_above, p_below)
    )
    from_below = step(p_above, "y", 1)
    from_above = step(p_below, "y", -1)
    from_far = step(added(p_far, from_z).astype(BF16), "y", 2)
    from_near = step(added(p_near, from_below_z, from_above_z).astype(BF16), "zl", 1)
    tokens = tokens + swap(tokens, 0, 3)
    [attended] = halves(functools.partial(place_kernel, kv_heads), side, (own_att, from_sib), (resp_q,), "place")
    from_far, from_near, from_below, from_above, attended, tokens = tie(
        (from_far, from_near, from_below, from_above, attended, tokens)
    )
    total = added(p_own, from_below, from_above, from_far, from_near)
    pass_on = jnp.concatenate([total[rows:pair], total[pair + rows :]], axis=0).astype(BF16)
    passed = step(pass_on, "core", 1)
    grad_q, grad_rk, grad_rv, grad_pk, grad_pv = halves(
        functools.partial(finish_kernel, kv_heads, float(slots * devices)),
        side,
        (own_grad, from_sib, total, passed, tokens),
        (resp_q, resp_k, resp_v, prompt_k, prompt_v),
        "finish",
    )
    return attended, grad_q, grad_rk, grad_rv, grad_pk, grad_pv


def solution(mesh):
    parts = Mesh(mesh.devices.reshape(4, 4, 4, 2, 2), ("x", "zh", "y", "zl", "core"))
    group, member = ("x", "zh"), ("y", "zl", "core")
    rank3, rank4, rank2 = P(group, member, None), P(group, member, None, None), P(group, member)
    return jax.shard_map(
        body,
        mesh=parts,
        in_specs=(rank3, rank3, rank4, rank4, rank4, rank4, rank2, rank2),
        out_specs=(rank4, rank4, rank4, rank4, rank3, rank3),
        check_vma=False,
    )
```
